128 devices in a mesh: ctx: 16 (over x, y), tp: 8 (over z, core).
Axes of the slice: x: 4, y: 4, z: 4, core: 2. Of those that a mesh axis runs over, the one named last changes fastest.
Arguments:
- rotated_queries: bfloat16 [8192, 8192], P('ctx', 'tp'), may hold values from -25 to 25
- rotated_keys: bfloat16 [8192, 1024], P('ctx', 'tp'), may hold values from -25 to 25
- value_matrix: bfloat16 [8192, 1024], P('ctx', 'tp'), may hold values from -6 to 6
- out_weight: bfloat16 [8192, 8192], P('tp', 'ctx'), may hold values from -0.0625 to 0.0625
- doc_ids: int32 [8192], replicated, may hold values from 0 to 7, never falling along the last dimension, each value on 1 to 2048 neighbouring positions
- assignment: int32 [16, 16], replicated, may hold values from 0 to 15, each once within a row
Outputs:
- owner_output: bfloat16 [8192, 8192], P('ctx', 'tp')
The draws below stay inside these ranges and needn't reach their ends.
Inputs may be any that keep to these rules, and one draw needn't show every extreme that they name: Each row of assignment is a permutation of 0 to 15. `doc_ids`: documents are numbered in order along the tokens; each has 1 to 2048 tokens and one has exactly 2048.
All inputs are finite; a program needn't handle non-finite values.
Results may differ from the reference program's by a relative error of at most 0.017.
Values may be sent and summed in bfloat16 or wider, within the bound.
No kernel may reach another device: no remote copies, remote signals or barrier semaphores. Data moves between devices by JAX's collectives and lax.ppermute only.
A program may use at most 320 MiB of HBM per device.

```python
import math
import jax
import jax.numpy as jnp
import numpy as np
from jax import lax

D = 8192
QUERY_HEADS = 64
KEY_VALUE_HEADS = 8
HEAD_WIDTH = 128
TOKENS_PER_SHARD = 512
QUERY_PER_KV = 8
PACKED_TOKENS = 8192
OWNERS = 16
QB = 32
NDOC = 8
MAXLEN = 2048
N_TP = 8


def draw_rotated_keys(key, part):
    key = jax.random.fold_in(key, 11)
    final_output = jnp.clip(jax.random.normal(key, (PACKED_TOKENS, KEY_VALUE_HEADS * HEAD_WIDTH), jnp.float32), -4.0, 4.0)
    return final_output.astype(jnp.bfloat16)


def draw_rotated_queries(key, part):
    key = jax.random.fold_in(key, 23)
    final_output = jnp.clip(jax.random.normal(key, (PACKED_TOKENS, QUERY_HEADS * HEAD_WIDTH), jnp.float32), -4.0, 4.0)
    return final_output.astype(jnp.bfloat16)


def block_scale(rng, dims, pieces, low, top_value):
    def one(axis_at, shards_of):
        draws = jax.random.uniform(jax.random.fold_in(jax.random.fold_in(rng, 6), axis_at), (shards_of,), jnp.float32, low / len(pieces), top_value / len(pieces))
        return jnp.repeat(jnp.exp(draws), dims[axis_at] // shards_of).reshape((-1,) + (1,) * (len(dims) - axis_at - 1))

    level = one(*pieces[0])
    for cut in pieces[1:]:
        level = level * one(*cut)
    return level


def profile(count, total, limit, skew):
    loads = [(1 << 20) // math.isqrt(grade ** skew) + 1 for grade in range(2, count + 1)]
    surplus, given = total - limit - (count - 1), [1] * (count - 1)
    while surplus > 0:
        free = [i for i in range(count - 1) if given[i] < limit]
        pool, budget = sum([loads[i] for i in free]), surplus
        for i in free:
            more = min(limit - given[i], max(1, budget * loads[i] // pool), surplus)
            given[i] = given[i] + more
            surplus = surplus - more
    return np.array([limit] + given)


def uneven(key, count, total, reach, skew):
    if count == 2:
        one = jax.random.randint(key, (), max(1, total - reach), min(reach, total - 1) + 1)
        return jnp.stack([one, total - one])
    sizes = jnp.asarray(profile(count, total, reach, skew), jnp.int32)
    pairs = (count - 1) // 2
    donor, sink = sizes[1:1 + 2 * pairs:2], sizes[2:2 + 2 * pairs:2]
    room = jnp.minimum(donor - 1, reach - sink)
    moved = jax.random.randint(jax.random.fold_in(key, 1), (pairs,), 0, 1 << 20) % (room + 1)
    sizes = sizes.at[1:1 + 2 * pairs:2].set(donor - moved).at[2:2 + 2 * pairs:2].set(sink + moved)
    return sizes[jax.random.permutation(jax.random.fold_in(key, 2), count)]


def normal_values(key, dims, deviation, reach, pieces=(), held_as=jnp.bfloat16):
    array = deviation * jax.random.normal(key, dims, jnp.float32)
    if pieces:
        array = array * block_scale(key, dims, pieces, -0.22, 0.18)
    return jnp.clip(array, -reach, reach).astype(held_as)


def setup_inputs(seed: int = 0) -> dict:
    splits = jax.random.split(jax.random.key(seed), 7)
    return {
        "rotated_queries": draw_rotated_queries(jax.random.fold_in(splits[6], 71), 0),
        "rotated_keys": draw_rotated_keys(jax.random.fold_in(splits[6], 71), 0),
        "value_matrix": normal_values(splits[2], (PACKED_TOKENS, KEY_VALUE_HEADS * HEAD_WIDTH), 1.0, 6.0, ((0, 16), (1, 8))),
        "out_weight": normal_values(splits[3], (QUERY_HEADS * HEAD_WIDTH, D), (QUERY_HEADS * HEAD_WIDTH) ** -0.5, 0.0625, ((0, 8), (1, 16))),
        "doc_ids": jnp.searchsorted(jnp.cumsum(uneven(splits[4], NDOC, PACKED_TOKENS, MAXLEN, 2)), jnp.arange(PACKED_TOKENS), side="right").astype(jnp.int32),
        "assignment": jax.vmap(lambda own: jax.random.permutation(own, OWNERS))(jax.random.split(splits[5], OWNERS)).reshape((OWNERS, OWNERS)).astype(jnp.int32),
    }


def reference(rotated_queries, rotated_keys, value_matrix, out_weight, doc_ids, assignment):
    scale = 1.0 / math.sqrt(HEAD_WIDTH)
    positions = jnp.arange(PACKED_TOKENS, dtype=jnp.int32)
    number_blocks = PACKED_TOKENS // TOKENS_PER_SHARD
    query_tensor_five = rotated_queries.reshape(number_blocks, TOKENS_PER_SHARD, KEY_VALUE_HEADS, QUERY_PER_KV, HEAD_WIDTH)
    key_tensor_three = rotated_keys.astype(jnp.float32).reshape(PACKED_TOKENS, KEY_VALUE_HEADS, HEAD_WIDTH)
    value_tensor_three = value_matrix.astype(jnp.float32).reshape(PACKED_TOKENS, KEY_VALUE_HEADS, HEAD_WIDTH)

    def head_split(head_index):
        head_keys = lax.dynamic_index_in_dim(key_tensor_three, head_index, 1, keepdims=False)
        head_values = lax.dynamic_index_in_dim(value_tensor_three, head_index, 1, keepdims=False)

        def per_block(block_index):
            block_queries = query_tensor_five[block_index, :, head_index].astype(jnp.float32)
            block_pos = block_index * TOKENS_PER_SHARD + jnp.arange(TOKENS_PER_SHARD, dtype=jnp.int32)
            block_doc = lax.dynamic_slice_in_dim(doc_ids, block_index * TOKENS_PER_SHARD, TOKENS_PER_SHARD)
            scores = jnp.einsum('tgd,sd->tgs', block_queries, head_keys) * scale
            visible = (block_doc[:, None] == doc_ids[None, :]) & (positions[None, :] <= block_pos[:, None])
            visible = visible[:, None, :]
            row_max = lax.optimization_barrier(jnp.max(jnp.where(visible, scores, -jnp.inf), axis=-1, keepdims=True))
            exp_terms = jnp.where(visible, jnp.exp(scores - row_max), 0.0)
            denominator = lax.optimization_barrier(jnp.sum(exp_terms, axis=-1))
            weights = lax.optimization_barrier(exp_terms.astype(jnp.bfloat16)).astype(jnp.float32)
            numerator = jnp.einsum('tgs,sd->tgd', weights, head_values)
            return (numerator / denominator[..., None]).astype(jnp.bfloat16)
        return lax.map(per_block, jnp.arange(number_blocks, dtype=jnp.int32))
    attention_output = lax.map(head_split, jnp.arange(KEY_VALUE_HEADS, dtype=jnp.int32))
    attention_output = jnp.transpose(attention_output, (1, 2, 0, 3, 4)).reshape(PACKED_TOKENS, QUERY_HEADS * HEAD_WIDTH)
    columns = QUERY_HEADS * HEAD_WIDTH // N_TP
    projected = jnp.zeros((PACKED_TOKENS, D), jnp.float32)
    for split_index in range(N_TP):
        product = jnp.dot(attention_output[:, split_index * columns:(split_index + 1) * columns], out_weight[split_index * columns:(split_index + 1) * columns], preferred_element_type=jnp.float32)
        projected = projected + lax.optimization_barrier(product.astype(jnp.bfloat16)).astype(jnp.float32)
    projected = projected.astype(jnp.bfloat16)
    source_base = jnp.arange(number_blocks, dtype=jnp.int32) * TOKENS_PER_SHARD
    order = source_base[None, :, None] + jnp.transpose(assignment)[:, :, None] * QB + jnp.arange(QB, dtype=jnp.int32)[None, None, :]
    return jnp.take(projected, order.reshape(-1).astype(jnp.int32), axis=0)
```

```python
import functools
import math

import jax
import jax.numpy as jnp
from jax import lax
from jax.experimental import pallas as pl
from jax.experimental.pallas import tpu as pltpu
from jax.sharding import PartitionSpec as P

HEAD_WIDTH = 128
NDOC = 8
SIDE = 4
LOG2E = 1.4426950408889634
TILE = 128
CHUNK = 512


def ctx_shift(steps):
    return [(i, (i + steps) % 16) for i in range(16)]


def grid_shift(dx, dy):
    return [
        (4 * x + y, 4 * ((x + dx) % 4) + (y + dy) % 4) for x in range(4) for y in range(4)
    ]


def z_shift(steps):
    return [(t, (t + 2 * steps) % 8) for t in range(8)]


CORES = [(t, t ^ 1) for t in range(8)]


def attend_kernel(bounds_ref, q_ref, start_ref, *rest):
    parts = rest[:5]
    out_ref, window, stacked, scores, top, total, acc = rest[5:]
    step = pl.program_id(0)
    span = parts[0].shape[0]
    tokens = q_ref.shape[0]
    heads = q_ref.shape[1] // HEAD_WIDTH

    @pl.when(step == 0)
    def _():
        for k in range(5):
            window[pl.ds(k * span, span), :] = parts[k][...]

    for h in range(heads):
        stacked[pl.ds(h * tokens, tokens), :] = q_ref[:, h * HEAD_WIDTH : (h + 1) * HEAD_WIDTH]
    first = 4 * span + step * tokens
    low = bounds_ref[0, step] // CHUNK
    full = (first + 1) // CHUNK
    high = (first + tokens - 1) // CHUNK + 1
    plain = jnp.clip((bounds_ref[1, step] + CHUNK - 1) // CHUNK, low, full)
    top[...] = jnp.full_like(top, -1e30)

    def score(chunk, masked):
        keys = window[pl.ds(pl.multiple_of(chunk * CHUNK, CHUNK), CHUNK), :HEAD_WIDTH]
        s = lax.dot_general(
            stacked[...], keys, (((1,), (1,)), ((), ())), preferred_element_type=jnp.float32
        )
        if masked:
            there = lax.broadcasted_iota(jnp.int32, (tokens, CHUNK), 1) + chunk * CHUNK
            here = lax.broadcasted_iota(jnp.int32, (tokens, CHUNK), 0) + first
            seen = (there >= start_ref[...]) & (there <= here)
            s = jnp.where(seen[None], s.reshape(heads, tokens, CHUNK), -1e30)
            s = s.reshape(heads * tokens, CHUNK)
        scores[chunk] = s
        best = top[...]
        for g in range(CHUNK // 128):
            best = jnp.maximum(best, s[:, g * 128 : (g + 1) * 128])
        top[...] = best

    lax.fori_loop(low, plain, lambda i, _: score(i, True), None)
    lax.fori_loop(plain, full, lambda i, _: score(i, False), None)
    lax.fori_loop(full, high, lambda i, _: score(i, True), None)

    top[...] = jnp.broadcast_to(jnp.max(top[...], axis=1, keepdims=True), top.shape)
    total[...] = jnp.zeros_like(total)
    acc[...] = jnp.zeros_like(acc)

    def weigh(chunk, _):
        pieces, run, peak = [], total[...], top[...]
        for g in range(CHUNK // 128):
            s = scores[chunk, :, g * 128 : (g + 1) * 128]
            e = jnp.exp2((s - peak) * (LOG2E / math.sqrt(HEAD_WIDTH)))
            run = run + e
            pieces.append(e.astype(jnp.bfloat16))
        total[...] = run
        values = window[pl.ds(pl.multiple_of(chunk * CHUNK, CHUNK), CHUNK), HEAD_WIDTH:]
        acc[...] += jnp.dot(
            jnp.concatenate(pieces, axis=1), values, preferred_element_type=jnp.float32
        )

    lax.fori_loop(low, high, weigh, None)
    result = acc[...] / jnp.sum(total[...], axis=1, keepdims=True)
    for h in range(heads):
        out_ref[:, h * HEAD_WIDTH : (h + 1) * HEAD_WIDTH] = result[
            h * tokens : (h + 1) * tokens
        ].astype(out_ref.dtype)


def attend(queries, parts, starts, bounds):
    tokens, width = queries.shape
    span = parts[0].shape[0]
    rows = TILE * width // HEAD_WIDTH
    return pl.pallas_call(
        attend_kernel,
        grid_spec=pltpu.PrefetchScalarGridSpec(
            num_scalar_prefetch=1,
            grid=(tokens // TILE,),
            in_specs=[
                pl.BlockSpec((TILE, width), lambda i, b: (i, 0)),
                pl.BlockSpec((TILE, 1), lambda i, b: (i, 0)),
            ]
            + [pl.BlockSpec((span, 2 * HEAD_WIDTH), lambda i, b: (0, 0))] * 5,
            out_specs=pl.BlockSpec((TILE, width), lambda i, b: (i, 0)),
            scratch_shapes=[
                pltpu.VMEM((5 * span, 2 * HEAD_WIDTH), jnp.bfloat16),
                pltpu.VMEM((rows, HEAD_WIDTH), jnp.bfloat16),
                pltpu.VMEM((5 * span // CHUNK, rows, CHUNK), jnp.float32),
                pltpu.VMEM((rows, 128), jnp.float32),
                pltpu.VMEM((rows, 128), jnp.float32),
                pltpu.VMEM((rows, 128), jnp.float32),
            ],
        ),
        out_shape=jax.ShapeDtypeStruct((tokens, width), jnp.bfloat16),
        compiler_params=pltpu.CompilerParams(vmem_limit_bytes=40 * 1024 * 1024),
        cost_estimate=pl.CostEstimate(
            flops=8 * 10**9, bytes_accessed=4 * 10**6, transcendentals=8 * 10**6
        ),
    )(bounds, queries, starts, *parts)


def document_starts(doc_ids, me, tokens):
    docs = jnp.arange(NDOC, dtype=jnp.int32)
    first = jnp.sum((doc_ids[None, :] < docs[:, None]).astype(jnp.int32), axis=1)
    mine = lax.dynamic_slice_in_dim(doc_ids, me * tokens, tokens)
    starts = jnp.sum(jnp.where(mine[:, None] == docs[None, :], first[None, :], 0), axis=1)
    starts = starts - (me - 4) * tokens
    tiles = starts.reshape(-1, TILE)
    return starts[:, None], jnp.stack([tiles[:, 0], tiles[:, -1]])


def project_kernel(turn_ref, a_ref, b_ref, *rest):
    weights, outs = rest[:SIDE], rest[SIDE:]
    half = a_ref.shape[1]
    for e in range(SIDE):
        pick = lax.rem(turn_ref[0] + e, SIDE)
        for d in range(SIDE):

            @pl.when(pick == d)
            def _():
                r = jnp.dot(a_ref[...], weights[d][:half], preferred_element_type=jnp.float32)
                r = r + jnp.dot(b_ref[...], weights[d][half:], preferred_element_type=jnp.float32)
                outs[e][...] = r.astype(outs[e].dtype)


def project(turn, mine, partner, weights):
    rows = mine.shape[0]
    cols = weights[0].shape[1]
    out = jax.ShapeDtypeStruct((rows, cols), jnp.bfloat16)
    vmem = pl.BlockSpec(memory_space=pltpu.VMEM)
    return pl.pallas_call(
        project_kernel,
        in_specs=[pl.BlockSpec(memory_space=pltpu.SMEM)] + [vmem] * (2 + SIDE),
        out_specs=[vmem] * SIDE,
        out_shape=[out] * SIDE,
        compiler_params=pltpu.CompilerParams(vmem_limit_bytes=32 * 1024 * 1024),
        cost_estimate=pl.CostEstimate(
            flops=2 * rows * 2 * mine.shape[1] * cols * SIDE,
            bytes_accessed=10**7,
            transcendentals=0,
        ),
    )(turn, mine, partner, *weights)


def add(a, b):
    return (a.astype(jnp.float32) + b.astype(jnp.float32)).astype(jnp.bfloat16)


def reduce_z(pieces):
    here, ahead, across, behind = pieces
    cut = here.shape[0] // 2
    up = lax.ppermute(across[:cut], "tp", z_shift(1))
    down = lax.ppermute(across[cut:], "tp", z_shift(-1))
    ahead = jnp.concatenate([add(ahead[:cut], up), ahead[cut:]])
    behind = jnp.concatenate([behind[:cut], add(behind[cut:], down)])
    from_below = lax.ppermute(ahead, "tp", z_shift(1))
    from_above = lax.ppermute(behind, "tp", z_shift(-1))
    return (
        here.astype(jnp.float32)
        + from_below.astype(jnp.float32)
        + from_above.astype(jnp.float32)
    ).astype(jnp.bfloat16)


def shards(rotated_queries, rotated_keys, value_matrix, out_weight, doc_ids, assignment):
    me, lane = lax.axis_index("ctx"), lax.axis_index("tp")
    x, y = me // SIDE, me % SIDE
    z, core = lane // 2, lane % 2
    tokens = rotated_queries.shape[0]
    owners = lax.axis_size("ctx")
    block = tokens // owners
    part = out_weight.shape[1] // 2

    both = jnp.concatenate([rotated_keys, value_matrix], axis=1)
    window = [lax.ppermute(both, "ctx", ctx_shift(k)) for k in (4, 3, 2, 1)] + [both]
    starts, bounds = document_starts(doc_ids, me, tokens)

    kept = lax.dynamic_slice_in_dim(out_weight, core * part, part, axis=1)
    given = lax.dynamic_slice_in_dim(out_weight, (1 - core) * part, part, axis=1)
    pooled = jnp.concatenate([kept, lax.ppermute(given, "tp", CORES)], axis=0)
    w_next = lax.ppermute(pooled, "ctx", grid_shift(-1, 0))
    w_across = lax.ppermute(w_next, "ctx", grid_shift(-1, 0))
    late, _ = lax.optimization_barrier((pooled, window[0]))
    w_last = lax.ppermute(late, "ctx", grid_shift(1, 0))
    weights = [pooled, w_next, w_across, w_last]
    turn = ((z - x) % SIDE).reshape(1)

    attended = attend(rotated_queries, window, starts, bounds)

    def finish(mine):
        partner = lax.ppermute(mine, "tp", CORES)
        return reduce_z(project(turn, mine, partner, weights))

    a_next = lax.ppermute(attended, "ctx", grid_shift(0, -1))
    a_last = lax.ppermute(attended, "ctx", grid_shift(0, 1))
    cut = tokens // 2
    a_low = lax.ppermute(a_next[:cut], "ctx", grid_shift(0, -1))
    a_high = lax.ppermute(a_last[cut:], "ctx", grid_shift(0, 1))
    reduced = [finish(attended), finish(a_next), finish(a_low), finish(a_high), finish(a_last)]

    blocks = jnp.concatenate(reduced).reshape(SIDE * owners, block, part)
    sources = lax.dynamic_slice_in_dim(assignment, x * SIDE, SIDE, axis=0)
    turned = (jnp.arange(SIDE, dtype=jnp.int32) - y) % SIDE
    order = (turned[:, None] * owners + sources).T
    outgoing = jnp.take(blocks, order.reshape(-1), axis=0).reshape(owners, SIDE, block, part)
    arrived = lax.all_to_all(outgoing, "ctx", split_axis=0, concat_axis=0, tiled=True)
    arrived = arrived.reshape(SIDE, 2, 2, SIDE, block, part)
    stay = lax.dynamic_index_in_dim(arrived, core, 1, keepdims=False)
    leave = lax.dynamic_index_in_dim(arrived, 1 - core, 1, keepdims=False)
    came = lax.ppermute(leave, "tp", CORES)
    low = jnp.where(core == 0, stay, came)
    high = jnp.where(core == 0, came, stay)
    out = jnp.stack([low, high], axis=2)
    return out.transpose(0, 3, 4, 1, 2, 5).reshape(tokens, 4 * part)


def solution(mesh):
    placed = (P("ctx", "tp"), P("ctx", "tp"), P("ctx", "tp"), P("tp", "ctx"), P(), P())
    return jax.shard_map(
        shards, mesh=mesh, in_specs=placed, out_specs=P("ctx", "tp"), check_vma=False
    )
```

```python
import functools
import math

import jax
import jax.numpy as jnp
from jax import lax
from jax.experimental import pallas as pl
from jax.experimental.pallas import tpu as pltpu
from jax.sharding import PartitionSpec as P

HEAD_WIDTH = 128
NDOC = 8
SIDE = 4
SCALE = math.log2(math.e) / math.sqrt(HEAD_WIDTH)
TILE = 256
GROUP = 4


def grid_shift(dx, dy):
    return [
        (4 * x + y, 4 * ((x + dx) % 4) + (y + dy) % 4) for x in range(4) for y in range(4)
    ]


def z_shift(steps):
    return [(t, (t + 2 * steps) % 8) for t in range(8)]


CORES = [(t, t ^ 1) for t in range(8)]


def attend_kernel(firsts_ref, q_ref, *rest):
    parts = rest[:5]
    outs, (window, stacked, top, total, acc) = rest[5:-5], rest[-5:]
    step = pl.program_id(0)
    span = parts[0].shape[0]
    tokens = q_ref.shape[0]
    heads = q_ref.shape[1] // HEAD_WIDTH

    @pl.when(step == 0)
    def _():
        for k in range(5):
            window[pl.ds(k * span, span), :] = parts[k][...]

    for h in range(heads):
        stacked[pl.ds(h * tokens, tokens), :] = q_ref[:, h * HEAD_WIDTH : (h + 1) * HEAD_WIDTH]
    first = 4 * span + step * tokens

    def beginning(position):
        at = firsts_ref[0]
        for d in range(1, NDOC):
            at = jnp.where(position >= firsts_ref[d], firsts_ref[d], at)
        return at

    low = beginning(first) // tokens
    full = first // tokens
    plain = jnp.clip((beginning(first + tokens - 1) + tokens - 1) // tokens, low, full)
    begins = beginning(first + lax.broadcasted_iota(jnp.int32, (tokens, 1), 0))
    top[...] = jnp.full_like(top, -1e30)
    total[...] = jnp.zeros_like(total)
    acc[...] = jnp.zeros_like(acc)

    def absorb(start, size, masked):
        place = pl.ds(pl.multiple_of(start, tokens), size)
        keys, values = window[place, :HEAD_WIDTH], window[place, HEAD_WIDTH:]
        if masked:
            there = lax.broadcasted_iota(jnp.int32, (tokens, size), 1) + start
            here = lax.broadcasted_iota(jnp.int32, (tokens, size), 0) + first
            seen = (there >= begins) & (there <= here)
        for g in range(heads // GROUP):
            rows = slice(g * GROUP * tokens, (g + 1) * GROUP * tokens)
            s = lax.dot_general(
                stacked[rows], keys, (((1,), (1,)), ((), ())), preferred_element_type=jnp.float32
            )
            if masked:
                s = jnp.where(seen[None], s.reshape(GROUP, tokens, size), -1e30)
                s = s.reshape(GROUP * tokens, size)
            old = top[rows]
            new = jnp.maximum(old, jnp.max(s, axis=1, keepdims=True))
            peak = jnp.maximum(new, -1e29)
            fade = jnp.exp2((old - peak) * SCALE)
            run, pieces = total[rows] * fade, []
            for k in range(size // 128):
                e = jnp.exp2((s[:, k * 128 : (k + 1) * 128] - peak) * SCALE)
                run = run + e
                pieces.append(e.astype(jnp.bfloat16))
            top[rows] = new
            total[rows] = run
            acc[rows] = acc[rows] * fade + jnp.dot(
                jnp.concatenate(pieces, axis=1), values, preferred_element_type=jnp.float32
            )

    def sweep(begin, end, masked):
        pairs = (end - begin) // 2
        lax.fori_loop(
            0, pairs, lambda i, _: absorb((begin + 2 * i) * tokens, 2 * tokens, masked), None
        )

        @pl.when((end - begin) % 2 == 1)
        def _():
            absorb((end - 1) * tokens, tokens, masked)

    sweep(low, plain, True)
    sweep(plain, full, False)
    absorb(first, tokens, True)
    result = acc[...] / jnp.sum(total[...], axis=1, keepdims=True)
    for k in range(len(outs)):

        @pl.when(step == k)
        def _():
            for h in range(heads):
                outs[k][:, h * HEAD_WIDTH : (h + 1) * HEAD_WIDTH] = result[
                    h * tokens : (h + 1) * tokens
                ].astype(outs[k].dtype)


def attend(queries, parts, firsts):
    tokens, width = queries.shape
    span = parts[0].shape[0]
    rows = TILE * width // HEAD_WIDTH
    return pl.pallas_call(
        attend_kernel,
        grid_spec=pltpu.PrefetchScalarGridSpec(
            num_scalar_prefetch=1,
            grid=(tokens // TILE,),
            in_specs=[
                pl.BlockSpec((TILE, width), lambda i, b: (i, 0)),
            ]
            + [pl.BlockSpec((span, 2 * HEAD_WIDTH), lambda i, b: (0, 0))] * 5,
            out_specs=[pl.BlockSpec((TILE, width), lambda i, b: (0, 0))] * (tokens // TILE),
            scratch_shapes=[
                pltpu.VMEM((5 * span, 2 * HEAD_WIDTH), jnp.bfloat16),
                pltpu.VMEM((rows, HEAD_WIDTH), jnp.bfloat16),
                pltpu.VMEM((rows, 128), jnp.float32),
                pltpu.VMEM((rows, 128), jnp.float32),
                pltpu.VMEM((rows, 128), jnp.float32),
            ],
        ),
        out_shape=[jax.ShapeDtypeStruct((TILE, width), jnp.bfloat16)] * (tokens // TILE),
        compiler_params=pltpu.CompilerParams(vmem_limit_bytes=24 * 1024 * 1024),
        cost_estimate=pl.CostEstimate(
            flops=1, bytes_accessed=1, transcendentals=0
        ),
    )(firsts, queries, *parts)


def document_starts(doc_ids, me, tokens):
    docs = jnp.arange(NDOC, dtype=jnp.int32)
    first = jnp.sum((doc_ids[None, :] < docs[:, None]).astype(jnp.int32), axis=1)
    return first - (me - 4) * tokens


def project_kernel(count, turn_ref, *refs):
    mine, partner = refs[:count], refs[count : 2 * count]
    weights, rest = refs[2 * count : 2 * count + 2 * SIDE], refs[2 * count + 2 * SIDE :]
    *arrays, held = rest
    if len(arrays) > SIDE:
        arrays[-1][...] = sum_of(arrays[:SIDE])
        arrays = arrays[SIDE:-1]
    for d in range(SIDE):
        row = 0
        for a, b in zip(mine, partner):
            r = jnp.dot(a[...], weights[2 * d][...], preferred_element_type=jnp.float32)
            r += jnp.dot(b[...], weights[2 * d + 1][...], preferred_element_type=jnp.float32)
            held[d, row : row + a.shape[0]] = r.astype(held.dtype)
            row += a.shape[0]
    for e in range(SIDE):
        arrays[e][...] = held[lax.rem(turn_ref[0] + e, SIDE)]


def sum_of(terms):
    r = terms[0][...].astype(jnp.float32)
    for t in terms[1:]:
        r += t[...].astype(jnp.float32)
    return r.astype(terms[0].dtype)


def project(turn, mine, partner, weights, finished):
    count = len(mine)
    rows = sum(a.shape[0] for a in mine)
    out = jax.ShapeDtypeStruct((rows, weights[0].shape[1]), jnp.bfloat16)
    vmem = pl.BlockSpec(memory_space=pltpu.VMEM)
    number = SIDE + (1 if finished else 0)
    outs = pl.pallas_call(
        functools.partial(project_kernel, count),
        in_specs=[pl.BlockSpec(memory_space=pltpu.SMEM)]
        + [vmem] * (2 * count + 2 * SIDE + len(finished)),
        out_specs=[vmem] * number,
        out_shape=[out] * number,
        scratch_shapes=[pltpu.VMEM((SIDE,) + out.shape, out.dtype)],
        compiler_params=pltpu.CompilerParams(vmem_limit_bytes=10 * 1024 * 1024),
        cost_estimate=pl.CostEstimate(flops=1, bytes_accessed=1, transcendentals=0),
    )(turn, *mine, *partner, *weights, *finished)
    return outs[:SIDE], outs[SIDE:]


def after(value, *others):
    return lax.optimization_barrier((value,) + others)[0]


def meet(*groups):
    flat = lax.optimization_barrier(tuple(a for g in groups for a in g))
    out, at = [], 0
    for g in groups:
        out.append(list(flat[at : at + len(g)]))
        at += len(g)
    return out


def spread_z(pieces):
    return [pieces[0]] + [lax.ppermute(pieces[e], "tp", z_shift(e)) for e in range(1, SIDE)]


def collect_kernel(y_ref, sources_ref, *refs):
    *terms, out_ref, held = refs
    groups = [terms[:1], terms[1:2], terms[2 : 2 + SIDE], terms[2 + SIDE :]]
    block = out_ref.shape[2]
    half = terms[0].shape[0] // 2
    places = (((0, 0), (0, 8)), ((1, 0), (3, 8)), ((1, 8), (3, 0)), ((2, 0), (2, 8)))
    for group, pair in zip(groups, places):
        r = sum_of(group)
        for k, (d, first) in enumerate(pair):
            for b in range(half // block):
                row = k * half + b * block
                held[d, first + b] = r[row : row + block]
    for source in range(SIDE):
        d = lax.rem(source - y_ref[0] + SIDE, SIDE)
        for o in range(out_ref.shape[0]):
            out_ref[o, source] = held[d, sources_ref[source, o]]


def collect(y, sources, own, outer, inner, far):
    terms = [*own, *outer, *inner, *far]
    rows, part = terms[0].shape
    owners = sources.shape[1]
    block = rows // owners
    smem = pl.BlockSpec(memory_space=pltpu.SMEM)
    shape = (owners, SIDE, block, part)
    return pl.pallas_call(
        collect_kernel,
        grid=(1,),
        in_specs=[smem] * 2 + [pl.BlockSpec((rows, part), lambda i: (0, 0))] * len(terms),
        out_specs=pl.BlockSpec(shape, lambda i: (0, 0, 0, 0)),
        out_shape=jax.ShapeDtypeStruct(shape, jnp.bfloat16),
        scratch_shapes=[pltpu.VMEM((SIDE, owners, block, part), jnp.bfloat16)],
        compiler_params=pltpu.CompilerParams(vmem_limit_bytes=16 * 1024 * 1024),
        cost_estimate=pl.CostEstimate(flops=1, bytes_accessed=1, transcendentals=0),
    )(y, sources, *terms)


def assemble_kernel(core_ref, here_ref, swapped_ref, out_ref):
    block, part = here_ref.shape[-2:]
    for core in range(2):

        @pl.when(core_ref[0] == core)
        def _():
            for x in range(SIDE):
                for source in range(SIDE):
                    row = (x * SIDE + source) * block
                    for p in range(2):
                        stay = here_ref[x, core, p, source]
                        came = swapped_ref[x, p, source]
                        for c, piece in ((core, stay), (1 - core, came)):
                            col = (2 * p + c) * part
                            out_ref[row : row + block, col : col + part] = piece


def assemble(core, here, swapped):
    block, part = here.shape[-2:]
    vmem = pl.BlockSpec(memory_space=pltpu.VMEM)
    return pl.pallas_call(
        assemble_kernel,
        in_specs=[pl.BlockSpec(memory_space=pltpu.SMEM)] + [vmem] * 2,
        out_specs=vmem,
        out_shape=jax.ShapeDtypeStruct((SIDE * SIDE * block, 4 * part), jnp.bfloat16),
        compiler_params=pltpu.CompilerParams(vmem_limit_bytes=8 * 1024 * 1024),
        cost_estimate=pl.CostEstimate(flops=1, bytes_accessed=1, transcendentals=0),
    )(core, here, swapped)


def shards(rotated_queries, rotated_keys, value_matrix, out_weight, doc_ids, assignment):
    me, lane = lax.axis_index("ctx"), lax.axis_index("tp")
    x, y = me // SIDE, me % SIDE
    z, core = lane // 2, lane % 2
    tokens = rotated_queries.shape[0]
    owners = lax.axis_size("ctx")
    block = tokens // owners
    part = out_weight.shape[1] // 2

    both = jnp.concatenate([rotated_keys, value_matrix], axis=1)
    above = lax.ppermute(both, "ctx", grid_shift(1, 0))
    near = [
        lax.ppermute(jnp.where(y + k < SIDE, both, above), "ctx", grid_shift(0, k))
        for k in range(1, SIDE)
    ]
    firsts = document_starts(doc_ids, me, tokens)

    kept = lax.dynamic_slice_in_dim(out_weight, core * part, part, axis=1)
    given = lax.dynamic_slice_in_dim(out_weight, (1 - core) * part, part, axis=1)
    taken = lax.ppermute(given, "tp", CORES)
    kept_next, taken_next = [lax.ppermute(a, "ctx", grid_shift(-1, 0)) for a in (kept, taken)]
    taken_last, kept_last = [lax.ppermute(a, "ctx", grid_shift(1, 0)) for a in (taken, kept)]
    near, (kept_next, taken_last) = meet(near, [kept_next, taken_last])
    kept_far = lax.ppermute(kept_next, "ctx", grid_shift(-1, 0))
    taken_far = lax.ppermute(taken_last, "ctx", grid_shift(1, 0))
    weights = [kept, taken, kept_next, taken_next, kept_far, taken_far, kept_last, taken_last]
    turn = ((z - x) % SIDE).reshape(1)
    window = [above] + near[::-1] + [both]

    def swap(a):
        return lax.ppermute(a, "tp", CORES)

    def along(a, steps):
        return lax.ppermute(a, "ctx", grid_shift(0, -steps))

    def terms(mine, partner=None, finished=()):
        partner = partner or [swap(a) for a in mine]
        pieces, total = project(turn, mine, partner, weights, finished)
        return spread_z(pieces), total

    head, tail = attend(rotated_queries, window, firsts)
    (head, tail), weights = meet([head, tail], weights)
    swaps = [swap(head), swap(tail)]
    outer = [along(head, 1), along(tail, 3)]
    own, _ = terms([head, tail], swaps)
    outer, pair, _ = meet(outer, [tail, head], own[:1])
    inner = [along(pair[0], 1), along(pair[1], 3)]
    outer_terms, _ = terms(outer)
    inner, outer, own, _ = meet(inner, outer, own, outer_terms[:1])
    far = [along(outer[0], 1), along(outer[1], 3)]
    inner_terms, own = terms(inner, finished=own)
    far, outer_terms, _ = meet(far, outer_terms, inner_terms[:1])
    far_terms, outer = terms(far, finished=outer_terms)
    inner_terms, far_terms = meet(inner_terms, far_terms)
    sources = lax.dynamic_slice_in_dim(assignment, x * SIDE, SIDE, axis=0)
    outgoing = collect(y.reshape(1), sources, own, outer, inner_terms, far_terms)
    arrived = lax.all_to_all(outgoing, "ctx", split_axis=0, concat_axis=0, tiled=True)
    arrived = arrived.reshape(SIDE, 2, 2, SIDE, block, part)
    leave = lax.dynamic_index_in_dim(arrived, 1 - core, 1, keepdims=False)
    return assemble(core.reshape(1), arrived, swap(leave))


def solution(mesh):
    placed = (P("ctx", "tp"), P("ctx", "tp"), P("ctx", "tp"), P("tp", "ctx"), P(), P())
    return jax.shard_map(
        shards, mesh=mesh, in_specs=placed, out_specs=P("ctx", "tp"), check_vma=False
    )
```

```python
import functools
import math

import jax
import jax.numpy as jnp
from jax import lax
from jax.experimental import pallas as pl
from jax.experimental.pallas import tpu as pltpu
from jax.sharding import PartitionSpec as P

HEAD_WIDTH = 128
NDOC = 8
SIDE = 4
SCALE = math.log2(math.e) / math.sqrt(HEAD_WIDTH)
TILE = 256
GROUP = 4


def grid_shift(dx, dy):
    return [
        (4 * x + y, 4 * ((x + dx) % 4) + (y + dy) % 4) for x in range(4) for y in range(4)
    ]


def z_shift(steps):
    return [(t, (t + 2 * steps) % 8) for t in range(8)]


CORES = [(t, t ^ 1) for t in range(8)]


def attend_kernel(firsts_ref, q_ref, *rest):
    parts = rest[:5]
    outs, (window, stacked, top, total, acc) = rest[5:-5], rest[-5:]
    step = pl.program_id(0)
    span = parts[0].shape[0]
    tokens = q_ref.shape[0]
    heads = q_ref.shape[1] // HEAD_WIDTH

    @pl.when(step == 0)
    def _():
        for k in range(5):
            window[pl.ds(k * span, span), :] = parts[k][...]

    for h in range(heads):
        stacked[pl.ds(h * tokens, tokens), :] = q_ref[:, h * HEAD_WIDTH : (h + 1) * HEAD_WIDTH]
    first = 4 * span + step * tokens

    def beginning(position):
        at = firsts_ref[0]
        for d in range(1, NDOC):
            at = jnp.where(position >= firsts_ref[d], firsts_ref[d], at)
        return at

    low = beginning(first) // tokens
    full = first // tokens
    plain = jnp.clip((beginning(first + tokens - 1) + tokens - 1) // tokens, low, full)
    begins = beginning(first + lax.broadcasted_iota(jnp.int32, (tokens, 1), 0))
    top[...] = jnp.full_like(top, -1e30)
    total[...] = jnp.zeros_like(total)
    acc[...] = jnp.zeros_like(acc)

    def absorb(start, size, masked):
        place = pl.ds(pl.multiple_of(start, tokens), size)
        keys, values = window[place, :HEAD_WIDTH], window[place, HEAD_WIDTH:]
        if masked:
            there = lax.broadcasted_iota(jnp.int32, (tokens, size), 1) + start
            here = lax.broadcasted_iota(jnp.int32, (tokens, size), 0) + first
            seen = (there >= begins) & (there <= here)
        for g in range(heads // GROUP):
            rows = slice(g * GROUP * tokens, (g + 1) * GROUP * tokens)
            s = lax.dot_general(
                stacked[rows], keys, (((1,), (1,)), ((), ())), preferred_element_type=jnp.float32
            )
            if masked:
                s = jnp.where(seen[None], s.reshape(GROUP, tokens, size), -1e30)
                s = s.reshape(GROUP * tokens, size)
            old = top[rows]
            new = jnp.maximum(old, jnp.max(s, axis=1, keepdims=True))
            peak = jnp.maximum(new, -1e29)
            fade = jnp.exp2((old - peak) * SCALE)
            run, pieces = total[rows] * fade, []
            for k in range(size // 128):
                e = jnp.exp2((s[:, k * 128 : (k + 1) * 128] - peak) * SCALE)
                run = run + e
                pieces.append(e.astype(jnp.bfloat16))
            top[rows] = new
            total[rows] = run
            acc[rows] = acc[rows] * fade + jnp.dot(
                jnp.concatenate(pieces, axis=1), values, preferred_element_type=jnp.float32
            )

    def sweep(begin, end, masked):
        pairs = (end - begin) // 2
        lax.fori_loop(
            0, pairs, lambda i, _: absorb((begin + 2 * i) * tokens, 2 * tokens, masked), None
        )

        @pl.when((end - begin) % 2 == 1)
        def _():
            absorb((end - 1) * tokens, tokens, masked)

    sweep(low, plain, True)
    sweep(plain, full, False)
    absorb(first, tokens, True)
    result = acc[...] / jnp.sum(total[...], axis=1, keepdims=True)
    for k in range(len(outs)):

        @pl.when(step == k)
        def _():
            for h in range(heads):
                outs[k][:, h * HEAD_WIDTH : (h + 1) * HEAD_WIDTH] = result[
                    h * tokens : (h + 1) * tokens
                ].astype(outs[k].dtype)


def attend(queries, parts, firsts):
    tokens, width = queries.shape
    span = parts[0].shape[0]
    rows = TILE * width // HEAD_WIDTH
    return pl.pallas_call(
        attend_kernel,
        grid_spec=pltpu.PrefetchScalarGridSpec(
            num_scalar_prefetch=1,
            grid=(tokens // TILE,),
            in_specs=[
                pl.BlockSpec((TILE, width), lambda i, b: (i, 0)),
            ]
            + [pl.BlockSpec((span, 2 * HEAD_WIDTH), lambda i, b: (0, 0))] * 5,
            out_specs=[pl.BlockSpec((TILE, width), lambda i, b: (0, 0))] * (tokens // TILE),
            scratch_shapes=[
                pltpu.VMEM((5 * span, 2 * HEAD_WIDTH), jnp.bfloat16),
                pltpu.VMEM((rows, HEAD_WIDTH), jnp.bfloat16),
                pltpu.VMEM((rows, 128), jnp.float32),
                pltpu.VMEM((rows, 128), jnp.float32),
                pltpu.VMEM((rows, 128), jnp.float32),
            ],
        ),
        out_shape=[jax.ShapeDtypeStruct((TILE, width), jnp.bfloat16)] * (tokens // TILE),
        compiler_params=pltpu.CompilerParams(vmem_limit_bytes=65300 * 1024),
        cost_estimate=pl.CostEstimate(
            flops=1, bytes_accessed=1, transcendentals=0
        ),
    )(firsts, queries, *parts)


def document_starts(doc_ids, me, tokens):
    docs = jnp.arange(NDOC, dtype=jnp.int32)
    first = jnp.sum((doc_ids[None, :] < docs[:, None]).astype(jnp.int32), axis=1)
    return first - (me - 4) * tokens


def project_kernel(count, turn_ref, *refs):
    mine, partner = refs[:count], refs[count : 2 * count]
    weights, rest = refs[2 * count : 2 * count + 2 * SIDE], refs[2 * count + 2 * SIDE :]
    *arrays, held = rest
    if len(arrays) > SIDE:
        arrays[-1][...] = sum_of(arrays[:SIDE])
        arrays = arrays[SIDE:-1]
    for d in range(SIDE):
        row = 0
        for a, b in zip(mine, partner):
            r = jnp.dot(a[...], weights[2 * d][...], preferred_element_type=jnp.float32)
            r += jnp.dot(b[...], weights[2 * d + 1][...], preferred_element_type=jnp.float32)
            held[d, row : row + a.shape[0]] = r.astype(held.dtype)
            row += a.shape[0]
    for e in range(SIDE):
        arrays[e][...] = held[lax.rem(turn_ref[0] + e, SIDE)]


def sum_of(terms):
    r = terms[0][...].astype(jnp.float32)
    for t in terms[1:]:
        r += t[...].astype(jnp.float32)
    return r.astype(terms[0].dtype)


def project(turn, mine, partner, weights, finished):
    count = len(mine)
    rows = sum(a.shape[0] for a in mine)
    out = jax.ShapeDtypeStruct((rows, weights[0].shape[1]), jnp.bfloat16)
    vmem = pl.BlockSpec(memory_space=pltpu.VMEM)
    number = SIDE + (1 if finished else 0)
    outs = pl.pallas_call(
        functools.partial(project_kernel, count),
        in_specs=[pl.BlockSpec(memory_space=pltpu.SMEM)]
        + [vmem] * (2 * count + 2 * SIDE + len(finished)),
        out_specs=[vmem] * number,
        out_shape=[out] * number,
        scratch_shapes=[pltpu.VMEM((SIDE,) + out.shape, out.dtype)],
        compiler_params=pltpu.CompilerParams(vmem_limit_bytes=10 * 1024 * 1024),
        cost_estimate=pl.CostEstimate(flops=1, bytes_accessed=1, transcendentals=0),
    )(turn, *mine, *partner, *weights, *finished)
    return outs[:SIDE], outs[SIDE:]


def after(value, *others):
    return lax.optimization_barrier((value,) + others)[0]


def meet(*groups):
    flat = lax.optimization_barrier(tuple(a for g in groups for a in g))
    out, at = [], 0
    for g in groups:
        out.append(list(flat[at : at + len(g)]))
        at += len(g)
    return out


def spread_z(pieces):
    return [pieces[0]] + [lax.ppermute(pieces[e], "tp", z_shift(e)) for e in range(1, SIDE)]


def collect_kernel(y_ref, sources_ref, *refs):
    *terms, out_ref, held = refs
    groups = [terms[:1], terms[1:2], terms[2 : 2 + SIDE], terms[2 + SIDE :]]
    block = out_ref.shape[2]
    half = terms[0].shape[0] // 2
    places = (((0, 0), (0, 8)), ((1, 0), (3, 8)), ((1, 8), (3, 0)), ((2, 0), (2, 8)))
    for group, pair in zip(groups, places):
        r = sum_of(group)
        for k, (d, first) in enumerate(pair):
            for b in range(half // block):
                row = k * half + b * block
                held[d, first + b] = r[row : row + block]
    for source in range(SIDE):
        d = lax.rem(source - y_ref[0] + SIDE, SIDE)
        for o in range(out_ref.shape[0]):
            out_ref[o, source] = held[d, sources_ref[source, o]]


def collect(y, sources, own, outer, inner, far):
    terms = [*own, *outer, *inner, *far]
    rows, part = terms[0].shape
    owners = sources.shape[1]
    block = rows // owners
    smem = pl.BlockSpec(memory_space=pltpu.SMEM)
    shape = (owners, SIDE, block, part)
    return pl.pallas_call(
        collect_kernel,
        grid=(1,),
        in_specs=[smem] * 2 + [pl.BlockSpec((rows, part), lambda i: (0, 0))] * len(terms),
        out_specs=pl.BlockSpec(shape, lambda i: (0, 0, 0, 0)),
        out_shape=jax.ShapeDtypeStruct(shape, jnp.bfloat16),
        scratch_shapes=[pltpu.VMEM((SIDE, owners, block, part), jnp.bfloat16)],
        compiler_params=pltpu.CompilerParams(vmem_limit_bytes=60 * 1024 * 1024),
        cost_estimate=pl.CostEstimate(flops=1, bytes_accessed=1, transcendentals=0),
    )(y, sources, *terms)


def assemble_kernel(core_ref, here_ref, swapped_ref, out_ref):
    block, part = here_ref.shape[-2:]
    for core in range(2):

        @pl.when(core_ref[0] == core)
        def _():
            for x in range(SIDE):
                for source in range(SIDE):
                    row = (x * SIDE + source) * block
                    for p in range(2):
                        stay = here_ref[x, core, p, source]
                        came = swapped_ref[x, p, source]
                        for c, piece in ((core, stay), (1 - core, came)):
                            col = (2 * p + c) * part
                            out_ref[row : row + block, col : col + part] = piece


def assemble(core, here, swapped):
    block, part = here.shape[-2:]
    vmem = pl.BlockSpec(memory_space=pltpu.VMEM)
    return pl.pallas_call(
        assemble_kernel,
        in_specs=[pl.BlockSpec(memory_space=pltpu.SMEM)] + [vmem] * 2,
        out_specs=vmem,
        out_shape=jax.ShapeDtypeStruct((SIDE * SIDE * block, 4 * part), jnp.bfloat16),
        compiler_params=pltpu.CompilerParams(vmem_limit_bytes=8 * 1024 * 1024),
        cost_estimate=pl.CostEstimate(flops=1, bytes_accessed=1, transcendentals=0),
    )(core, here, swapped)


def shards(rotated_queries, rotated_keys, value_matrix, out_weight, doc_ids, assignment):
    me, lane = lax.axis_index("ctx"), lax.axis_index("tp")
    x, y = me // SIDE, me % SIDE
    z, core = lane // 2, lane % 2
    tokens = rotated_queries.shape[0]
    owners = lax.axis_size("ctx")
    block = tokens // owners
    part = out_weight.shape[1] // 2

    both = jnp.concatenate([rotated_keys, value_matrix], axis=1)
    above = lax.ppermute(both, "ctx", grid_shift(1, 0))
    near = [
        lax.ppermute(jnp.where(y + k < SIDE, both, above), "ctx", grid_shift(0, k))
        for k in range(1, SIDE)
    ]
    firsts = document_starts(doc_ids, me, tokens)

    kept = lax.dynamic_slice_in_dim(out_weight, core * part, part, axis=1)
    given = lax.dynamic_slice_in_dim(out_weight, (1 - core) * part, part, axis=1)
    taken = lax.ppermute(given, "tp", CORES)
    kept_next, taken_next = [lax.ppermute(a, "ctx", grid_shift(-1, 0)) for a in (kept, taken)]
    taken_last = lax.ppermute(after(taken, above), "ctx", grid_shift(1, 0))
    kept_last = lax.ppermute(after(kept, above), "ctx", grid_shift(1, 0))
    near, (kept_next, taken_last) = meet(near, [kept_next, taken_last])
    kept_far = lax.ppermute(kept_next, "ctx", grid_shift(-1, 0))
    taken_far = lax.ppermute(taken_last, "ctx", grid_shift(1, 0))
    weights = [kept, taken, kept_next, taken_next, kept_far, taken_far, kept_last, taken_last]
    turn = ((z - x) % SIDE).reshape(1)
    window = [above] + near[::-1] + [both]

    def swap(a):
        return lax.ppermute(a, "tp", CORES)

    def along(a, steps):
        return lax.ppermute(a, "ctx", grid_shift(0, -steps))

    def terms(mine, partner=None, finished=()):
        partner = partner or [swap(a) for a in mine]
        pieces, total = project(turn, mine, partner, weights, finished)
        return spread_z(pieces), total

    head, tail = attend(rotated_queries, window, firsts)
    (head, tail), weights = meet([head, tail], weights)
    swaps = [swap(head), swap(tail)]
    outer = [along(head, 1), along(tail, 3)]
    own, _ = terms([head, tail], swaps)
    outer, pair, _ = meet(outer, [tail, head], own[:1] + own[2:3])
    inner = [along(pair[0], 1), along(pair[1], 3)]
    outer_terms, _ = terms(outer)
    inner, outer, own, _ = meet(inner, outer, own, outer_terms[:1] + outer_terms[2:3])
    far = [along(outer[0], 1), along(outer[1], 3)]
    inner_terms, own = terms(inner, finished=own)
    far, outer_terms, _ = meet(far, outer_terms, inner_terms[:1])
    far_terms, outer = terms(far, finished=outer_terms)
    inner_terms, far_terms = meet(inner_terms, far_terms)
    sources = lax.dynamic_slice_in_dim(assignment, x * SIDE, SIDE, axis=0)
    outgoing = collect(y.reshape(1), sources, own, outer, inner_terms, far_terms)
    arrived = lax.all_to_all(outgoing, "ctx", split_axis=0, concat_axis=0, tiled=True)
    arrived = arrived.reshape(SIDE, 2, 2, SIDE, block, part)
    leave = lax.dynamic_index_in_dim(arrived, 1 - core, 1, keepdims=False)
    return assemble(core.reshape(1), arrived, swap(leave))


def solution(mesh):
    placed = (P("ctx", "tp"), P("ctx", "tp"), P("ctx", "tp"), P("tp", "ctx"), P(), P())
    return jax.shard_map(
        shards, mesh=mesh, in_specs=placed, out_specs=P("ctx", "tp"), check_vma=False
    )
```

```python
import functools
import math

import jax
import jax.numpy as jnp
from jax import lax
from jax.experimental import pallas as pl
from jax.experimental.pallas import tpu as pltpu
from jax.sharding import PartitionSpec as P

HEAD_WIDTH = 128
NDOC = 8
SIDE = 4
SCALE = math.log2(math.e) / math.sqrt(HEAD_WIDTH)
TILE = 256
GROUP = 4


def grid_shift(dx, dy):
    return [
        (4 * x + y, 4 * ((x + dx) % 4) + (y + dy) % 4) for x in range(4) for y in range(4)
    ]


def z_shift(steps):
    return [(t, (t + 2 * steps) % 8) for t in range(8)]


CORES = [(t, t ^ 1) for t in range(8)]


def attend_kernel(firsts_ref, q_ref, *rest):
    parts = rest[:5]
    outs, (window, stacked, top, total, acc) = rest[5:-5], rest[-5:]
    step = pl.program_id(0)
    span = parts[0].shape[0]
    tokens = q_ref.shape[0]
    heads = q_ref.shape[1] // HEAD_WIDTH

    @pl.when(step == 0)
    def _():
        for k in range(5):
            window[pl.ds(k * span, span), :] = parts[k][...]

    for h in range(heads):
        stacked[pl.ds(h * tokens, tokens), :] = q_ref[:, h * HEAD_WIDTH : (h + 1) * HEAD_WIDTH]
    first = 4 * span + step * tokens

    def beginning(position):
        at = firsts_ref[0]
        for d in range(1, NDOC):
            at = jnp.where(position >= firsts_ref[d], firsts_ref[d], at)
        return at

    low = beginning(first) // tokens
    full = first // tokens
    plain = jnp.clip((beginning(first + tokens - 1) + tokens - 1) // tokens, low, full)
    begins = beginning(first + lax.broadcasted_iota(jnp.int32, (tokens, 1), 0))
    top[...] = jnp.full_like(top, -1e30)
    total[...] = jnp.zeros_like(total)
    acc[...] = jnp.zeros_like(acc)

    def absorb(start, size, masked):
        place = pl.ds(pl.multiple_of(start, tokens), size)
        keys, values = window[place, :HEAD_WIDTH], window[place, HEAD_WIDTH:]
        if masked:
            there = lax.broadcasted_iota(jnp.int32, (tokens, size), 1) + start
            here = lax.broadcasted_iota(jnp.int32, (tokens, size), 0) + first
            seen = (there >= begins) & (there <= here)
        for g in range(heads // GROUP):
            rows = slice(g * GROUP * tokens, (g + 1) * GROUP * tokens)
            s = lax.dot_general(
                stacked[rows], keys, (((1,), (1,)), ((), ())), preferred_element_type=jnp.float32
            )
            if masked:
                s = jnp.where(seen[None], s.reshape(GROUP, tokens, size), -1e30)
                s = s.reshape(GROUP * tokens, size)
            old = top[rows]
            new = jnp.maximum(old, jnp.max(s, axis=1, keepdims=True))
            peak = jnp.maximum(new, -1e29)
            fade = jnp.exp2((old - peak) * SCALE)
            run, pieces = total[rows] * fade, []
            for k in range(size // 128):
                e = jnp.exp2((s[:, k * 128 : (k + 1) * 128] - peak) * SCALE)
                run = run + e
                pieces.append(e.astype(jnp.bfloat16))
            top[rows] = new
            total[rows] = run
            acc[rows] = acc[rows] * fade + jnp.dot(
                jnp.concatenate(pieces, axis=1), values, preferred_element_type=jnp.float32
            )

    def sweep(begin, end, masked):
        pairs = (end - begin) // 2
        lax.fori_loop(
            0, pairs, lambda i, _: absorb((begin + 2 * i) * tokens, 2 * tokens, masked), None
        )

        @pl.when((end - begin) % 2 == 1)
        def _():
            absorb((end - 1) * tokens, tokens, masked)

    sweep(low, plain, True)
    sweep(plain, full, False)
    absorb(first, tokens, True)
    result = acc[...] / jnp.sum(total[...], axis=1, keepdims=True)
    for k in range(len(outs)):

        @pl.when(step == k)
        def _():
            for h in range(heads):
                outs[k][:, h * HEAD_WIDTH : (h + 1) * HEAD_WIDTH] = result[
                    h * tokens : (h + 1) * tokens
                ].astype(outs[k].dtype)


def attend(queries, parts, firsts):
    tokens, width = queries.shape
    span = parts[0].shape[0]
    rows = TILE * width // HEAD_WIDTH
    return pl.pallas_call(
        attend_kernel,
        grid_spec=pltpu.PrefetchScalarGridSpec(
            num_scalar_prefetch=1,
            grid=(tokens // TILE,),
            in_specs=[
                pl.BlockSpec((TILE, width), lambda i, b: (i, 0)),
            ]
            + [pl.BlockSpec((span, 2 * HEAD_WIDTH), lambda i, b: (0, 0))] * 5,
            out_specs=[pl.BlockSpec((TILE, width), lambda i, b: (0, 0))] * (tokens // TILE),
            scratch_shapes=[
                pltpu.VMEM((5 * span, 2 * HEAD_WIDTH), jnp.bfloat16),
                pltpu.VMEM((rows, HEAD_WIDTH), jnp.bfloat16),
                pltpu.VMEM((rows, 128), jnp.float32),
                pltpu.VMEM((rows, 128), jnp.float32),
                pltpu.VMEM((rows, 128), jnp.float32),
            ],
        ),
        out_shape=[jax.ShapeDtypeStruct((TILE, width), jnp.bfloat16)] * (tokens // TILE),
        compiler_params=pltpu.CompilerParams(vmem_limit_bytes=65300 * 1024),
        cost_estimate=pl.CostEstimate(
            flops=1, bytes_accessed=1, transcendentals=0
        ),
    )(firsts, queries, *parts)


def document_starts(doc_ids, me, tokens):
    docs = jnp.arange(NDOC, dtype=jnp.int32)
    first = jnp.sum((doc_ids[None, :] < docs[:, None]).astype(jnp.int32), axis=1)
    return first - (me - 4) * tokens


def project_kernel(count, turn_ref, *refs):
    mine, partner = refs[:count], refs[count : 2 * count]
    weights, rest = refs[2 * count : 2 * count + 2 * SIDE], refs[2 * count + 2 * SIDE :]
    *arrays, held = rest
    if len(arrays) > SIDE:
        arrays[-1][...] = sum_of(arrays[:SIDE])
        arrays = arrays[SIDE:-1]
    for d in range(SIDE):
        row = 0
        for a, b in zip(mine, partner):
            r = jnp.dot(a[...], weights[2 * d][...], preferred_element_type=jnp.float32)
            r += jnp.dot(b[...], weights[2 * d + 1][...], preferred_element_type=jnp.float32)
            held[d, row : row + a.shape[0]] = r.astype(held.dtype)
            row += a.shape[0]
    for e in range(SIDE):
        arrays[e][...] = held[lax.rem(turn_ref[0] + e, SIDE)]


def sum_of(terms):
    r = terms[0][...].astype(jnp.float32)
    for t in terms[1:]:
        r += t[...].astype(jnp.float32)
    return r.astype(terms[0].dtype)


def project(turn, mine, partner, weights, finished):
    count = len(mine)
    rows = sum(a.shape[0] for a in mine)
    out = jax.ShapeDtypeStruct((rows, weights[0].shape[1]), jnp.bfloat16)
    vmem = pl.BlockSpec(memory_space=pltpu.VMEM)
    number = SIDE + (1 if finished else 0)
    outs = pl.pallas_call(
        functools.partial(project_kernel, count),
        in_specs=[pl.BlockSpec(memory_space=pltpu.SMEM)]
        + [vmem] * (2 * count + 2 * SIDE + len(finished)),
        out_specs=[vmem] * number,
        out_shape=[out] * number,
        scratch_shapes=[pltpu.VMEM((SIDE,) + out.shape, out.dtype)],
        compiler_params=pltpu.CompilerParams(vmem_limit_bytes=10 * 1024 * 1024),
        cost_estimate=pl.CostEstimate(flops=1, bytes_accessed=1, transcendentals=0),
    )(turn, *mine, *partner, *weights, *finished)
    return outs[:SIDE], outs[SIDE:]


def after(value, *others):
    return lax.optimization_barrier((value,) + others)[0]


def meet(*groups):
    flat = lax.optimization_barrier(tuple(a for g in groups for a in g))
    out, at = [], 0
    for g in groups:
        out.append(list(flat[at : at + len(g)]))
        at += len(g)
    return out


def spread_z(pieces):
    return [pieces[0]] + [lax.ppermute(pieces[e], "tp", z_shift(e)) for e in range(1, SIDE)]


def collect_kernel(y_ref, sources_ref, *refs):
    *terms, out_ref, held = refs
    groups = [terms[:1], terms[1:2], terms[2 : 2 + SIDE], terms[2 + SIDE :]]
    block = out_ref.shape[2]
    half = terms[0].shape[0] // 2
    places = (((0, 0), (0, 8)), ((1, 0), (3, 8)), ((1, 8), (3, 0)), ((2, 0), (2, 8)))
    for group, pair in zip(groups, places):
        r = sum_of(group)
        for k, (d, first) in enumerate(pair):
            for b in range(half // block):
                row = k * half + b * block
                held[d, first + b] = r[row : row + block]
    for source in range(SIDE):
        d = lax.rem(source - y_ref[0] + SIDE, SIDE)
        for o in range(out_ref.shape[0]):
            out_ref[o, source] = held[d, sources_ref[source, o]]


def collect(y, sources, own, outer, inner, far):
    terms = [*own, *outer, *inner, *far]
    rows, part = terms[0].shape
    owners = sources.shape[1]
    block = rows // owners
    smem = pl.BlockSpec(memory_space=pltpu.SMEM)
    shape = (owners, SIDE, block, part)
    return pl.pallas_call(
        collect_kernel,
        grid=(1,),
        in_specs=[smem] * 2 + [pl.BlockSpec((rows, part), lambda i: (0, 0))] * len(terms),
        out_specs=pl.BlockSpec(shape, lambda i: (0, 0, 0, 0)),
        out_shape=jax.ShapeDtypeStruct(shape, jnp.bfloat16),
        scratch_shapes=[pltpu.VMEM((SIDE, owners, block, part), jnp.bfloat16)],
        compiler_params=pltpu.CompilerParams(vmem_limit_bytes=60 * 1024 * 1024),
        cost_estimate=pl.CostEstimate(flops=1, bytes_accessed=1, transcendentals=0),
    )(y, sources, *terms)


def assemble_kernel(core_ref, here_ref, swapped_ref, out_ref):
    block, part = here_ref.shape[-2:]
    for core in range(2):

        @pl.when(core_ref[0] == core)
        def _():
            for x in range(SIDE):
                for source in range(SIDE):
                    row = (x * SIDE + source) * block
                    for p in range(2):
                        stay = here_ref[x, core, p, source]
                        came = swapped_ref[x, p, source]
                        for c, piece in ((core, stay), (1 - core, came)):
                            col = (2 * p + c) * part
                            out_ref[row : row + block, col : col + part] = piece


def assemble(core, here, swapped):
    block, part = here.shape[-2:]
    vmem = pl.BlockSpec(memory_space=pltpu.VMEM)
    return pl.pallas_call(
        assemble_kernel,
        in_specs=[pl.BlockSpec(memory_space=pltpu.SMEM)] + [vmem] * 2,
        out_specs=vmem,
        out_shape=jax.ShapeDtypeStruct((SIDE * SIDE * block, 4 * part), jnp.bfloat16),
        compiler_params=pltpu.CompilerParams(vmem_limit_bytes=8 * 1024 * 1024),
        cost_estimate=pl.CostEstimate(flops=1, bytes_accessed=1, transcendentals=0),
    )(core, here, swapped)


def shards(rotated_queries, rotated_keys, value_matrix, out_weight, doc_ids, assignment):
    me, lane = lax.axis_index("ctx"), lax.axis_index("tp")
    x, y = me // SIDE, me % SIDE
    z, core = lane // 2, lane % 2
    tokens = rotated_queries.shape[0]
    owners = lax.axis_size("ctx")
    block = tokens // owners
    part = out_weight.shape[1] // 2

    both = jnp.concatenate([rotated_keys, value_matrix], axis=1)
    above = lax.ppermute(both, "ctx", grid_shift(1, 0))
    near = [
        lax.ppermute(jnp.where(y + k < SIDE, both, above), "ctx", grid_shift(0, k))
        for k in range(1, SIDE)
    ]
    firsts = document_starts(doc_ids, me, tokens)

    kept = lax.dynamic_slice_in_dim(out_weight, core * part, part, axis=1)
    given = lax.dynamic_slice_in_dim(out_weight, (1 - core) * part, part, axis=1)
    taken = lax.ppermute(given, "tp", CORES)
    kept_next, taken_next = [lax.ppermute(a, "ctx", grid_shift(-1, 0)) for a in (kept, taken)]
    taken_last = lax.ppermute(after(taken, above), "ctx", grid_shift(1, 0))
    kept_last = lax.ppermute(after(kept, above), "ctx", grid_shift(1, 0))
    near, (kept_next, taken_last) = meet(near, [kept_next, taken_last])
    kept_far = lax.ppermute(kept_next, "ctx", grid_shift(-1, 0))
    taken_far = lax.ppermute(taken_last, "ctx", grid_shift(1, 0))
    weights = [kept, taken, kept_next, taken_next, kept_far, taken_far, kept_last, taken_last]
    turn = ((z - x) % SIDE).reshape(1)
    window = [above] + near[::-1] + [both]

    def swap(a):
        return lax.ppermute(a, "tp", CORES)

    def along(a, steps):
        return lax.ppermute(a, "ctx", grid_shift(0, -steps))

    def terms(mine, partner=None, finished=()):
        partner = partner or [swap(a) for a in mine]
        pieces, total = project(turn, mine, partner, weights, finished)
        return spread_z(pieces), total

    head, tail = attend(rotated_queries, window, firsts)
    (head, tail), weights = meet([head, tail], weights)
    swaps = [swap(head), swap(tail)]
    outer = [along(head, 1), along(tail, 3)]
    own, _ = terms([head, tail], swaps)
    outer, pair, _ = meet(outer, [tail, head], own[:1] + own[2:3])
    inner = [along(pair[0], 1), along(pair[1], 3)]
    outer_terms, _ = terms(outer)
    inner, outer, own, _ = meet(inner, outer, own, outer_terms[:1] + outer_terms[2:3])
    far = [along(outer[0], 1), along(outer[1], 3)]
    inner_terms, own = terms(inner, finished=own)
    far, _ = meet(far, inner_terms[:1] + outer_terms[1:2])
    far_terms, outer = terms(far, finished=outer_terms)
    inner_terms, far_terms = meet(inner_terms, far_terms)
    sources = lax.dynamic_slice_in_dim(assignment, x * SIDE, SIDE, axis=0)
    outgoing = collect(y.reshape(1), sources, own, outer, inner_terms, far_terms)
    arrived = lax.all_to_all(outgoing, "ctx", split_axis=0, concat_axis=0, tiled=True)
    arrived = arrived.reshape(SIDE, 2, 2, SIDE, block, part)
    leave = lax.dynamic_index_in_dim(arrived, 1 - core, 1, keepdims=False)
    return assemble(core.reshape(1), arrived, swap(leave))


def solution(mesh):
    placed = (P("ctx", "tp"), P("ctx", "tp"), P("ctx", "tp"), P("tp", "ctx"), P(), P())
    return jax.shard_map(
        shards, mesh=mesh, in_specs=placed, out_specs=P("ctx", "tp"), check_vma=False
    )
```
